32 devices in a mesh: case: 2 (over x), leaf: 16 (over z, y, core).
Axes of the slice: x: 2, y: 2, z: 4, core: 2. Of those that a mesh axis runs over, the one named last changes fastest.
Arguments:
- fields: bfloat16 [512, 2, 128, 128], P(('case', 'leaf')), parts along dimension 0, may hold values from -6 to 6
- own_factor: bfloat16 [4, 512, 2, 128, 128], P(None, ('case', 'leaf')), parts along dimension 1, may hold values from -0.25 to 0.25
- partner_factor: bfloat16 [4, 512, 2, 128, 128], P(None, ('case', 'leaf')), parts along dimension 1, may hold values from -0.25 to 0.25
- near_blocks: bfloat16 [1024, 2, 128, 128], P(('case', 'leaf')), parts along dimension 0, may hold values from -0.375 to 0.375
- near_pairs: int32 [512, 2], P('leaf'), may hold values from 0 to 31, as said below
- near_count: int32 [16], P('leaf'), may hold values from 16 to 32, as said below
Outputs:
- scattered: bfloat16 [512, 2, 128, 128], P(('case', 'leaf')), parts along dimension 0
The draws below stay inside these ranges and needn't reach their ends.
There are 2 independent parts, one for each index of `case`. The reference program is written for one: setup_inputs(seed, part) draws one part's arguments, and reference() takes and returns one part's arrays. A program takes and returns all parts, laid end to end along the dimension named above; an argument that names none is the same for every part. Nothing has to cross between parts.
Inputs may be any that keep to these rules, and one draw needn't show every extreme that they name: `near_pairs`: column 0 is a box position 0 to 15. Column 1 always names an existing box: on the first device it is at least 8, on the last at most 23. `near_count`: some device has all 32 slots live.
All inputs are finite; a program needn't handle non-finite values.
Results may differ from the reference program's by a relative error of at most 0.0055.
Values may be sent and summed in bfloat16 or wider, within the bound.
A program may use at most 64 MiB of HBM per device.

```python
import jax
import jax.numpy as jnp
import numpy as np

BOX = 128
RHS = 128
BOX_DEV = 16
LEVELS = 4
HALF = 8
NEAR_DEV = 32
BOXES = 256
NEARS = 512
N_LEAF = 16


def draw_near_pairs(key, part):
    key = jax.random.fold_in(key, 11)
    first, second = jax.random.split(key)
    slots = jnp.arange(NEARS, dtype=jnp.int32)
    owner = slots // NEAR_DEV
    place = slots % NEAR_DEV
    targets = jax.random.randint(first, (NEARS,), 0, BOX_DEV, dtype=jnp.int32)
    lower = jnp.where(owner == 0, HALF, 0).astype(jnp.int32)
    upper = jnp.where(owner == N_LEAF - 1, HALF + BOX_DEV, BOX_DEV + 2 * HALF).astype(jnp.int32)
    spread = jax.random.randint(second, (NEARS,), 0, 1 << 20, dtype=jnp.int32)
    sources = lower + spread % (upper - lower)
    sources = jnp.where(place == 0, lower, sources)
    sources = jnp.where(place == 1, upper - 1, sources)
    return jnp.stack([targets, sources], axis=1).astype(jnp.int32)


def draw_near_count(key, part):
    key = jax.random.fold_in(key, 23)
    first, second = jax.random.split(key)
    counts = jax.random.randint(first, (N_LEAF,), NEAR_DEV // 2, NEAR_DEV + 1, dtype=jnp.int32)
    chosen = jax.random.randint(second, (), 0, N_LEAF, dtype=jnp.int32)
    return jnp.where(jnp.arange(N_LEAF, dtype=jnp.int32) == chosen, NEAR_DEV, counts).astype(jnp.int32)


def block_levels(rng, extent, shards, low, largest):
    loudness, own = 1.0, jax.random.fold_in(rng, 6)
    for dim, parts in shards:
        heights = jnp.exp(jax.random.uniform(jax.random.fold_in(own, dim), (parts,), jnp.float32, low / len(shards), largest / len(shards)))
        loudness = loudness * jnp.repeat(heights, extent[dim] // parts).reshape([-1 if axis == dim else 1 for axis in range(len(extent))])
    return loudness


def noise(rng, dims, width, reach, shards=(), kind=jnp.bfloat16):
    array = width * jax.random.normal(rng, dims, jnp.float32)
    if shards:
        array = array * block_levels(rng, dims, shards, -0.22, 0.18)
    return jnp.clip(array, -reach, reach).astype(kind)


def setup_inputs(seed: int = 0, part: int = 0) -> dict:
    keys = jax.random.split(jax.random.key(seed), 7)
    part_keys = jax.random.split(jax.random.fold_in(keys[6], part), 7)
    fields = noise(part_keys[0], (BOXES, 2, BOX, RHS), 1.0, 6.0, ((0, 16),))
    own_factor = noise(part_keys[1], (LEVELS, BOXES, 2, BOX, BOX), (4 * BOX) ** -0.5, 0.25, ((1, 16),))
    partner_factor = noise(part_keys[2], (LEVELS, BOXES, 2, BOX, BOX), (4 * BOX) ** -0.5, 0.25, ((1, 16),))
    near_blocks = noise(part_keys[3], (NEARS, 2, BOX, BOX), (2 * BOX) ** -0.5, 0.375, ((0, 16),))
    near_pairs = draw_near_pairs(jax.random.fold_in(keys[6], 71), part)
    near_count = draw_near_count(jax.random.fold_in(keys[6], 71), part)
    return dict(fields=fields, own_factor=own_factor, partner_factor=partner_factor, near_blocks=near_blocks, near_pairs=near_pairs, near_count=near_count)


def complex_apply(weight, vec):
    wr = weight[:, 0].astype(jnp.float32)
    wi = weight[:, 1].astype(jnp.float32)
    vr = vec[:, 0].astype(jnp.float32)
    vi = vec[:, 1].astype(jnp.float32)
    real = jnp.einsum('nij,njr->nir', wr, vr) - jnp.einsum('nij,njr->nir', wi, vi)
    imag = jnp.einsum('nij,njr->nir', wr, vi) + jnp.einsum('nij,njr->nir', wi, vr)
    return jnp.stack([real, imag], axis=1)


def reference(fields, own_factor, partner_factor, near_blocks, near_pairs, near_count):
    depth = int(N_LEAF).bit_length() - 1
    boxes = np.arange(BOXES)
    devs = boxes // BOX_DEV
    spots = boxes % BOX_DEV
    section = fields
    for level in range(LEVELS):
        bit = depth - 1 - level
        partner = ((devs ^ (1 << bit)) * BOX_DEV + spots).astype(np.int32)
        total = complex_apply(own_factor[level], section) + complex_apply(partner_factor[level], section[partner])
        section = total.astype(jnp.bfloat16)
    slots = jnp.arange(NEARS, dtype=jnp.int32)
    owner = slots // NEAR_DEV
    sources = (owner * BOX_DEV - HALF + near_pairs[:, 1]).astype(jnp.int32)
    targets = (owner * BOX_DEV + near_pairs[:, 0]).astype(jnp.int32)
    live = (slots % NEAR_DEV) < near_count[owner]
    products = complex_apply(near_blocks, fields[sources])
    products = jnp.where(live[:, None, None, None], products, jnp.float32(0.0))
    near = jax.ops.segment_sum(products, targets, num_segments=BOXES)
    return (section.astype(jnp.float32) + near).astype(jnp.bfloat16)
```

```python
import functools

import jax
import jax.numpy as jnp
from jax import lax
from jax.experimental import pallas as pl
from jax.experimental.pallas import tpu as pltpu
from jax.sharding import PartitionSpec as P

MESH = pl.DeviceIdType.MESH
WINDOW = 4
LAG = 1
SLOTS_STEP = 4
TARGETS_STEP = 2
ROWS = 32


def stacked(vec):
    vr, vi = vec[0], vec[1]
    return jnp.concatenate(
        [jnp.concatenate([vr, vi], axis=1), jnp.concatenate([-vi, vr], axis=1)], axis=0
    )


def wide(weight):
    return jnp.concatenate([weight[0], weight[1]], axis=1)


def kernel(
    devices,
    pairs_ref,
    count_ref,
    fields_ref,
    own_ref,
    partner_ref,
    blocks_ref,
    out_ref,
    extended,
    own,
    other,
    blocks,
    arrived,
    section,
    products,
    near,
    result,
    send_sem,
    recv_sem,
    halo_send,
    halo_recv,
    field_sem,
    own_sem,
    other_sem,
    block_sem,
    out_sem,
):
    levels, boxes = own_ref.shape[0], own_ref.shape[1]
    slots = blocks_ref.shape[0]
    reach = boxes // 2
    depth = devices.bit_length() - 1
    box, rhs = fields_ref.shape[2], fields_ref.shape[3]
    me = lax.axis_index("leaf")
    has_left, has_right = me > 0, me < devices - 1
    partners = []
    for level in range(levels):
        bit = 2 ** (depth - 1 - level)
        partners.append(jnp.where((me // bit) % 2 == 0, me + bit, me - bit))

    load_fields = pltpu.make_async_copy(
        fields_ref, extended.at[pl.ds(reach, boxes)], field_sem.at[0]
    )
    load_blocks = pltpu.make_async_copy(blocks_ref, blocks, block_sem.at[0])
    load_own = [
        pltpu.make_async_copy(own_ref.at[l], own.at[l], own_sem.at[l]) for l in range(levels)
    ]
    load_other = [
        pltpu.make_async_copy(partner_ref.at[l], other.at[l], other_sem.at[l])
        for l in range(levels)
    ]

    def hop(level, place):
        source = fields_ref.at[place] if level == 0 else section.at[level - 1, place]
        return pltpu.make_async_remote_copy(
            src_ref=source,
            dst_ref=arrived.at[level, place],
            send_sem=send_sem.at[level, place],
            recv_sem=recv_sem.at[level, place],
            device_id={"leaf": partners[level]},
            device_id_type=MESH,
        )

    to_right = pltpu.make_async_remote_copy(
        src_ref=fields_ref.at[pl.ds(boxes - reach, reach)],
        dst_ref=extended.at[pl.ds(0, reach)],
        send_sem=halo_send.at[0],
        recv_sem=halo_recv.at[0],
        device_id={"leaf": jnp.minimum(me + 1, devices - 1)},
        device_id_type=MESH,
    )
    to_left = pltpu.make_async_remote_copy(
        src_ref=fields_ref.at[pl.ds(0, reach)],
        dst_ref=extended.at[pl.ds(reach + boxes, reach)],
        send_sem=halo_send.at[1],
        recv_sem=halo_recv.at[1],
        device_id={"leaf": jnp.maximum(me - 1, 0)},
        device_id_type=MESH,
    )

    def store(place):
        return pltpu.make_async_copy(result.at[place], out_ref.at[place], out_sem.at[place])

    barrier = pltpu.get_barrier_semaphore()
    for level in range(levels):
        pl.semaphore_signal(
            barrier, inc=1, device_id={"leaf": partners[level]}, device_id_type=MESH
        )

    @pl.when(has_left)
    def _():
        pl.semaphore_signal(barrier, inc=1, device_id={"leaf": me - 1}, device_id_type=MESH)

    @pl.when(has_right)
    def _():
        pl.semaphore_signal(barrier, inc=1, device_id={"leaf": me + 1}, device_id_type=MESH)

    load_fields.start()
    for level in range(levels):
        load_own[level].start()
        load_other[level].start()
    load_blocks.start()

    neighbours = jnp.where(has_left, 1, 0) + jnp.where(has_right, 1, 0)
    pl.semaphore_wait(barrier, levels + neighbours)

    for place in range(min(WINDOW, boxes)):
        hop(0, place).start()

    @pl.when(has_right)
    def _():
        to_right.start()

    @pl.when(has_left)
    def _():
        to_left.start()

    load_fields.wait()

    first_product = 2
    first_sum = first_product + slots // SLOTS_STEP
    first_store = first_sum + 1
    steps = max(boxes + (levels - 1) * LAG, first_store + boxes // TARGETS_STEP)

    def step(k, carry):
        @pl.when(k + WINDOW < boxes)
        def _():
            hop(0, k + WINDOW).start()

        for level in range(levels):
            place = k - level * LAG

            @pl.when(place == 0)
            def _():
                load_own[level].wait()
                load_other[level].wait()

            @pl.when((place >= 0) & (place < boxes))
            def _():
                hop(level, place).wait_recv()
                here = extended[reach + place] if level == 0 else section[level - 1, place]
                there = arrived[level, place]
                weights = jnp.concatenate(
                    [wide(own[level, place]), wide(other[level, place])], axis=1
                )
                vectors = jnp.concatenate([stacked(here), stacked(there)], axis=0)
                total = jnp.dot(weights, vectors, preferred_element_type=jnp.float32)
                total = total.astype(jnp.bfloat16)
                section[level, place, 0] = total[:, :rhs]
                section[level, place, 1] = total[:, rhs:]
                if level + 1 < levels:
                    hop(level + 1, place).start()

        @pl.when(k == first_product)
        def _():
            load_blocks.wait()

            @pl.when(has_left)
            def _():
                to_right.wait_recv()

            @pl.when(has_right)
            def _():
                to_left.wait_recv()

        @pl.when((k >= first_product) & (k < first_sum))
        def _():
            for j in range(SLOTS_STEP):
                slot = (k - first_product) * SLOTS_STEP + j
                vec = extended[pairs_ref[slot, 1]]
                products[slot] = jnp.dot(
                    wide(blocks[slot]), stacked(vec), preferred_element_type=jnp.float32
                )

        @pl.when((k >= first_sum) & (k < first_sum + boxes // TARGETS_STEP))
        def _():
            count = count_ref[0]
            first = (k - first_sum) * TARGETS_STEP

            def chunk(c, carry):
                rows = pl.ds(pl.multiple_of(c * ROWS, ROWS), ROWS)
                sums = [jnp.zeros((ROWS, 2 * rhs), jnp.float32) for _ in range(TARGETS_STEP)]
                for slot in range(slots):
                    value = products[slot, rows, :]
                    target = pairs_ref[slot, 0]
                    for j in range(TARGETS_STEP):
                        live = (target == first + j) & (slot < count)
                        sums[j] = sums[j] + jnp.where(live, 1.0, 0.0) * value
                for j in range(TARGETS_STEP):
                    near[first + j, rows, :] = sums[j]
                return carry

            lax.fori_loop(0, box // ROWS, chunk, 0)

        @pl.when(k >= first_store)
        def _():
            for j in range(TARGETS_STEP):
                place = (k - first_store) * TARGETS_STEP + j

                @pl.when(place < boxes)
                def _():
                    for part in range(2):
                        total = section[levels - 1, place, part].astype(jnp.float32)
                        total = total + near[place, :, part * rhs : (part + 1) * rhs]
                        result[place, part] = total.astype(jnp.bfloat16)
                    store(place).start()

        return carry

    lax.fori_loop(0, steps, step, 0)

    def drain(place, carry):
        for level in range(levels):
            hop(level, place).wait_send()
        store(place).wait()
        return carry

    lax.fori_loop(0, boxes, drain, 0)

    @pl.when(has_right)
    def _():
        to_right.wait_send()

    @pl.when(has_left)
    def _():
        to_left.wait_send()


def per_device(fields, own_factor, partner_factor, near_blocks, near_pairs, near_count):
    levels, boxes, _, box, rhs = own_factor.shape[:4] + fields.shape[3:]
    slots = near_blocks.shape[0]
    devices = lax.axis_size("leaf")
    smem = pl.BlockSpec(memory_space=pltpu.SMEM)
    hbm = pl.BlockSpec(memory_space=pl.ANY)
    vector = (2, box, rhs)
    weight = (2, box, box)
    bf16, f32 = jnp.bfloat16, jnp.float32
    dma = pltpu.SemaphoreType.DMA
    products = levels * boxes * 2 + slots
    return pl.pallas_call(
        functools.partial(kernel, devices),
        out_shape=jax.ShapeDtypeStruct(fields.shape, bf16),
        in_specs=[smem, smem, hbm, hbm, hbm, hbm],
        out_specs=hbm,
        scratch_shapes=[
            pltpu.VMEM((2 * boxes,) + vector, bf16),
            pltpu.VMEM((levels, boxes) + weight, bf16),
            pltpu.VMEM((levels, boxes) + weight, bf16),
            pltpu.VMEM((slots,) + weight, bf16),
            pltpu.VMEM((levels, boxes) + vector, bf16),
            pltpu.VMEM((levels, boxes) + vector, bf16),
            pltpu.VMEM((slots, box, 2 * rhs), f32),
            pltpu.VMEM((boxes, box, 2 * rhs), f32),
            pltpu.VMEM((boxes,) + vector, bf16),
            dma((levels, boxes)),
            dma((levels, boxes)),
            dma((2,)),
            dma((2,)),
            dma((1,)),
            dma((levels,)),
            dma((levels,)),
            dma((1,)),
            dma((boxes,)),
        ],
        compiler_params=pltpu.CompilerParams(
            collective_id=0, has_side_effects=True, vmem_limit_bytes=56 * 2**20
        ),
        cost_estimate=pl.CostEstimate(
            flops=8 * products * box * box * rhs,
            bytes_accessed=(products * box * box + 2 * boxes * box * rhs) * 4,
            transcendentals=0,
        ),
    )(near_pairs, near_count, fields, own_factor, partner_factor, near_blocks)


def solution(mesh):
    in_specs = (
        P(("case", "leaf"), None, None, None),
        P(None, ("case", "leaf"), None, None, None),
        P(None, ("case", "leaf"), None, None, None),
        P(("case", "leaf"), None, None, None),
        P("leaf", None),
        P("leaf"),
    )
    out_specs = P(("case", "leaf"), None, None, None)
    return jax.shard_map(
        per_device, mesh=mesh, in_specs=in_specs, out_specs=out_specs, check_vma=False
    )
```

```python
import functools

import jax
import jax.numpy as jnp
from jax import lax
from jax.experimental import pallas as pl
from jax.experimental.pallas import tpu as pltpu
from jax.sharding import PartitionSpec as P

MESH = pl.DeviceIdType.MESH
WINDOW = 4
LAG = 4
SLOTS_STEP = 4
TARGETS_STEP = 2
ROWS = 32


def stacked(vec):
    vr, vi = vec[0], vec[1]
    return jnp.concatenate(
        [jnp.concatenate([vr, vi], axis=1), jnp.concatenate([-vi, vr], axis=1)], axis=0
    )


def wide(weight):
    return jnp.concatenate([weight[0], weight[1]], axis=1)


def kernel(
    devices,
    pairs_ref,
    count_ref,
    fields_ref,
    own_ref,
    partner_ref,
    blocks_ref,
    out_ref,
    extended,
    own,
    other,
    blocks,
    arrived,
    section,
    products,
    near,
    result,
    send_sem,
    recv_sem,
    halo_send,
    halo_recv,
    field_sem,
    own_sem,
    other_sem,
    block_sem,
    out_sem,
):
    levels, boxes = own_ref.shape[0], own_ref.shape[1]
    slots = blocks_ref.shape[0]
    reach = boxes // 2
    depth = devices.bit_length() - 1
    box, rhs = fields_ref.shape[2], fields_ref.shape[3]
    me = lax.axis_index("leaf")
    has_left, has_right = me > 0, me < devices - 1
    partners = []
    for level in range(levels):
        bit = 2 ** (depth - 1 - level)
        partners.append(jnp.where((me // bit) % 2 == 0, me + bit, me - bit))

    load_fields = pltpu.make_async_copy(
        fields_ref, extended.at[pl.ds(reach, boxes)], field_sem.at[0]
    )
    load_blocks = pltpu.make_async_copy(blocks_ref, blocks, block_sem.at[0])
    load_own = [
        pltpu.make_async_copy(own_ref.at[l], own.at[l], own_sem.at[l]) for l in range(levels)
    ]
    load_other = [
        pltpu.make_async_copy(partner_ref.at[l], other.at[l], other_sem.at[l])
        for l in range(levels)
    ]

    def hop(level, place):
        source = fields_ref.at[place] if level == 0 else section.at[level - 1, place]
        return pltpu.make_async_remote_copy(
            src_ref=source,
            dst_ref=arrived.at[level, place],
            send_sem=send_sem.at[level, place],
            recv_sem=recv_sem.at[level, place],
            device_id={"leaf": partners[level]},
            device_id_type=MESH,
        )

    to_right = pltpu.make_async_remote_copy(
        src_ref=fields_ref.at[pl.ds(boxes - reach, reach)],
        dst_ref=extended.at[pl.ds(0, reach)],
        send_sem=halo_send.at[0],
        recv_sem=halo_recv.at[0],
        device_id={"leaf": jnp.minimum(me + 1, devices - 1)},
        device_id_type=MESH,
    )
    to_left = pltpu.make_async_remote_copy(
        src_ref=fields_ref.at[pl.ds(0, reach)],
        dst_ref=extended.at[pl.ds(reach + boxes, reach)],
        send_sem=halo_send.at[1],
        recv_sem=halo_recv.at[1],
        device_id={"leaf": jnp.maximum(me - 1, 0)},
        device_id_type=MESH,
    )

    def store(place):
        return pltpu.make_async_copy(result.at[place], out_ref.at[place], out_sem.at[place])

    barrier = pltpu.get_barrier_semaphore()
    for level in range(levels):
        pl.semaphore_signal(
            barrier, inc=1, device_id={"leaf": partners[level]}, device_id_type=MESH
        )

    @pl.when(has_left)
    def _():
        pl.semaphore_signal(barrier, inc=1, device_id={"leaf": me - 1}, device_id_type=MESH)

    @pl.when(has_right)
    def _():
        pl.semaphore_signal(barrier, inc=1, device_id={"leaf": me + 1}, device_id_type=MESH)

    load_fields.start()
    for level in range(levels):
        load_own[level].start()
        load_other[level].start()
    load_blocks.start()

    neighbours = jnp.where(has_left, 1, 0) + jnp.where(has_right, 1, 0)
    pl.semaphore_wait(barrier, levels + neighbours)

    for place in range(min(WINDOW, boxes)):
        hop(0, place).start()

    @pl.when(has_right)
    def _():
        to_right.start()

    @pl.when(has_left)
    def _():
        to_left.start()

    load_fields.wait()

    first_product = 2
    first_sum = first_product + slots // SLOTS_STEP
    store_steps = boxes // TARGETS_STEP
    first_store = max(first_sum + 1, boxes + (levels - 1) * LAG - store_steps)
    steps = first_store + store_steps

    def step(k, carry):
        @pl.when(k + WINDOW < boxes)
        def _():
            hop(0, k + WINDOW).start()

        for level in range(levels):
            place = k - level * LAG

            @pl.when(place == 0)
            def _():
                load_own[level].wait()
                load_other[level].wait()

            @pl.when((place >= 0) & (place < boxes))
            def _():
                hop(level, place).wait_recv()
                here = extended[reach + place] if level == 0 else section[level - 1, place]
                there = arrived[level, place]
                weights = jnp.concatenate(
                    [wide(own[level, place]), wide(other[level, place])], axis=1
                )
                vectors = jnp.concatenate([stacked(here), stacked(there)], axis=0)
                total = jnp.dot(weights, vectors, preferred_element_type=jnp.float32)
                total = total.astype(jnp.bfloat16)
                section[level, place, 0] = total[:, :rhs]
                section[level, place, 1] = total[:, rhs:]
                if level + 1 < levels:
                    hop(level + 1, place).start()

        @pl.when(k == first_product)
        def _():
            load_blocks.wait()

            @pl.when(has_left)
            def _():
                to_right.wait_recv()

            @pl.when(has_right)
            def _():
                to_left.wait_recv()

        @pl.when((k >= first_product) & (k < first_sum))
        def _():
            for j in range(SLOTS_STEP):
                slot = (k - first_product) * SLOTS_STEP + j
                vec = extended[pairs_ref[1, slot]]
                products[slot] = jnp.dot(
                    wide(blocks[slot]), stacked(vec), preferred_element_type=jnp.float32
                )

        @pl.when((k >= first_sum) & (k < first_sum + boxes // TARGETS_STEP))
        def _():
            count = count_ref[0]
            first = (k - first_sum) * TARGETS_STEP

            def chunk(c, carry):
                rows = pl.ds(pl.multiple_of(c * ROWS, ROWS), ROWS)
                sums = [jnp.zeros((ROWS, 2 * rhs), jnp.float32) for _ in range(TARGETS_STEP)]
                for slot in range(slots):
                    value = products[slot, rows, :]
                    target = pairs_ref[0, slot]
                    for j in range(TARGETS_STEP):
                        live = (target == first + j) & (slot < count)
                        sums[j] = sums[j] + jnp.where(live, 1.0, 0.0) * value
                for j in range(TARGETS_STEP):
                    near[first + j, rows, :] = sums[j]
                return carry

            lax.fori_loop(0, box // ROWS, chunk, 0)

        @pl.when(k >= first_store)
        def _():
            for j in range(TARGETS_STEP):
                place = (k - first_store) * TARGETS_STEP + j

                @pl.when(place < boxes)
                def _():
                    for part in range(2):
                        total = section[levels - 1, place, part].astype(jnp.float32)
                        total = total + near[place, :, part * rhs : (part + 1) * rhs]
                        result[place, part] = total.astype(jnp.bfloat16)
                    store(place).start()

        return carry

    lax.fori_loop(0, steps, step, 0)

    def drain(place, carry):
        for level in range(levels):
            hop(level, place).wait_send()
        store(place).wait()
        return carry

    lax.fori_loop(0, boxes, drain, 0)

    @pl.when(has_right)
    def _():
        to_right.wait_send()

    @pl.when(has_left)
    def _():
        to_left.wait_send()


def per_device(fields, own_factor, partner_factor, near_blocks, near_pairs, near_count):
    levels, boxes, _, box, rhs = own_factor.shape[:4] + fields.shape[3:]
    slots = near_blocks.shape[0]
    devices = lax.axis_size("leaf")
    smem = pl.BlockSpec(memory_space=pltpu.SMEM)
    hbm = pl.BlockSpec(memory_space=pl.ANY)
    vector = (2, box, rhs)
    weight = (2, box, box)
    bf16, f32 = jnp.bfloat16, jnp.float32
    dma = pltpu.SemaphoreType.DMA
    products = levels * boxes * 2 + slots
    return pl.pallas_call(
        functools.partial(kernel, devices),
        out_shape=jax.ShapeDtypeStruct(fields.shape, bf16),
        in_specs=[smem, smem, hbm, hbm, hbm, hbm],
        out_specs=hbm,
        scratch_shapes=[
            pltpu.VMEM((2 * boxes,) + vector, bf16),
            pltpu.VMEM((levels, boxes) + weight, bf16),
            pltpu.VMEM((levels, boxes) + weight, bf16),
            pltpu.VMEM((slots,) + weight, bf16),
            pltpu.VMEM((levels, boxes) + vector, bf16),
            pltpu.VMEM((levels, boxes) + vector, bf16),
            pltpu.VMEM((slots, box, 2 * rhs), f32),
            pltpu.VMEM((boxes, box, 2 * rhs), f32),
            pltpu.VMEM((boxes,) + vector, bf16),
            dma((levels, boxes)),
            dma((levels, boxes)),
            dma((2,)),
            dma((2,)),
            dma((1,)),
            dma((levels,)),
            dma((levels,)),
            dma((1,)),
            dma((boxes,)),
        ],
        compiler_params=pltpu.CompilerParams(
            collective_id=0, has_side_effects=True, vmem_limit_bytes=56 * 2**20
        ),
        cost_estimate=pl.CostEstimate(
            flops=8 * products * box * box * rhs,
            bytes_accessed=(products * box * box + 2 * boxes * box * rhs) * 4,
            transcendentals=0,
        ),
    )(near_pairs.T, near_count, fields, own_factor, partner_factor, near_blocks)


def solution(mesh):
    in_specs = (
        P(("case", "leaf"), None, None, None),
        P(None, ("case", "leaf"), None, None, None),
        P(None, ("case", "leaf"), None, None, None),
        P(("case", "leaf"), None, None, None),
        P("leaf", None),
        P("leaf"),
    )
    out_specs = P(("case", "leaf"), None, None, None)
    return jax.shard_map(
        per_device, mesh=mesh, in_specs=in_specs, out_specs=out_specs, check_vma=False
    )
```

```python
import functools

import jax
import jax.numpy as jnp
from jax import lax
from jax.experimental import pallas as pl
from jax.experimental.pallas import tpu as pltpu
from jax.sharding import PartitionSpec as P

MESH = pl.DeviceIdType.MESH
WINDOW = 4
LAG = 4
SLOTS_STEP = 4
TARGETS_STEP = 4
ROWS = 32


def stacked(vec):
    vr, vi = vec[0], vec[1]
    return jnp.concatenate(
        [jnp.concatenate([vr, vi], axis=1), jnp.concatenate([-vi, vr], axis=1)], axis=0
    )


def wide(weight):
    return jnp.concatenate([weight[0], weight[1]], axis=1)


def kernel(
    devices,
    pairs_ref,
    count_ref,
    fields_ref,
    own_ref,
    partner_ref,
    blocks_ref,
    out_ref,
    extended,
    own,
    other,
    blocks,
    arrived,
    section,
    products,
    near,
    result,
    send_sem,
    recv_sem,
    halo_send,
    halo_recv,
    field_sem,
    own_sem,
    other_sem,
    block_sem,
    out_sem,
):
    levels, boxes = own_ref.shape[0], own_ref.shape[1]
    slots = blocks_ref.shape[0]
    reach = boxes // 2
    depth = devices.bit_length() - 1
    box, rhs = fields_ref.shape[2], fields_ref.shape[3]
    me = lax.axis_index("leaf")
    has_left, has_right = me > 0, me < devices - 1
    partners = []
    for level in range(levels):
        bit = 2 ** (depth - 1 - level)
        partners.append(jnp.where((me // bit) % 2 == 0, me + bit, me - bit))

    load_fields = pltpu.make_async_copy(
        fields_ref, extended.at[pl.ds(reach, boxes)], field_sem.at[0]
    )
    load_blocks = pltpu.make_async_copy(blocks_ref, blocks, block_sem.at[0])
    load_own = [
        pltpu.make_async_copy(own_ref.at[l], own.at[l], own_sem.at[l]) for l in range(levels)
    ]
    load_other = [
        pltpu.make_async_copy(partner_ref.at[l], other.at[l], other_sem.at[l])
        for l in range(levels)
    ]

    def hop(level, place):
        source = fields_ref.at[place] if level == 0 else section.at[level - 1, place]
        return pltpu.make_async_remote_copy(
            src_ref=source,
            dst_ref=arrived.at[level, place],
            send_sem=send_sem.at[level, place],
            recv_sem=recv_sem.at[level, place],
            device_id={"leaf": partners[level]},
            device_id_type=MESH,
        )

    to_right = pltpu.make_async_remote_copy(
        src_ref=fields_ref.at[pl.ds(boxes - reach, reach)],
        dst_ref=extended.at[pl.ds(0, reach)],
        send_sem=halo_send.at[0],
        recv_sem=halo_recv.at[0],
        device_id={"leaf": jnp.minimum(me + 1, devices - 1)},
        device_id_type=MESH,
    )
    to_left = pltpu.make_async_remote_copy(
        src_ref=fields_ref.at[pl.ds(0, reach)],
        dst_ref=extended.at[pl.ds(reach + boxes, reach)],
        send_sem=halo_send.at[1],
        recv_sem=halo_recv.at[1],
        device_id={"leaf": jnp.maximum(me - 1, 0)},
        device_id_type=MESH,
    )

    def store(place):
        return pltpu.make_async_copy(result.at[place], out_ref.at[place], out_sem.at[place])

    barrier = pltpu.get_barrier_semaphore()
    for level in range(levels):
        pl.semaphore_signal(
            barrier, inc=1, device_id={"leaf": partners[level]}, device_id_type=MESH
        )

    @pl.when(has_left)
    def _():
        pl.semaphore_signal(barrier, inc=1, device_id={"leaf": me - 1}, device_id_type=MESH)

    @pl.when(has_right)
    def _():
        pl.semaphore_signal(barrier, inc=1, device_id={"leaf": me + 1}, device_id_type=MESH)

    load_fields.start()
    for level in range(levels):
        load_own[level].start()
        load_other[level].start()
    load_blocks.start()

    neighbours = jnp.where(has_left, 1, 0) + jnp.where(has_right, 1, 0)
    pl.semaphore_wait(barrier, levels + neighbours)

    for place in range(min(WINDOW, boxes)):
        hop(0, place).start()

    @pl.when(has_right)
    def _():
        to_right.start()

    @pl.when(has_left)
    def _():
        to_left.start()

    load_fields.wait()

    first_product = 2
    first_sum = first_product + slots // SLOTS_STEP
    store_steps = boxes // TARGETS_STEP
    first_store = max(first_sum + 1, boxes + (levels - 1) * LAG - store_steps)
    steps = first_store + store_steps

    def step(k, carry):
        @pl.when(k + WINDOW < boxes)
        def _():
            hop(0, k + WINDOW).start()

        for level in range(levels):
            place = k - level * LAG

            @pl.when(place == 0)
            def _():
                load_own[level].wait()
                load_other[level].wait()

            @pl.when((place >= 0) & (place < boxes))
            def _():
                hop(level, place).wait_recv()
                here = extended[reach + place] if level == 0 else section[level - 1, place]
                there = arrived[level, place]
                weights = jnp.concatenate(
                    [wide(own[level, place]), wide(other[level, place])], axis=1
                )
                vectors = jnp.concatenate([stacked(here), stacked(there)], axis=0)
                total = jnp.dot(weights, vectors, preferred_element_type=jnp.float32)
                total = total.astype(jnp.bfloat16)
                section[level, place, 0] = total[:, :rhs]
                section[level, place, 1] = total[:, rhs:]
                if level + 1 < levels:
                    hop(level + 1, place).start()

        @pl.when(k == first_product)
        def _():
            load_blocks.wait()

            @pl.when(has_left)
            def _():
                to_right.wait_recv()

            @pl.when(has_right)
            def _():
                to_left.wait_recv()

        @pl.when((k >= first_product) & (k < first_sum))
        def _():
            for j in range(SLOTS_STEP):
                slot = (k - first_product) * SLOTS_STEP + j
                vec = extended[pairs_ref[1, slot]]
                products[slot] = jnp.dot(
                    wide(blocks[slot]), stacked(vec), preferred_element_type=jnp.float32
                )

        @pl.when((k >= first_sum) & (k < first_sum + boxes // TARGETS_STEP))
        def _():
            count = count_ref[0]
            first = (k - first_sum) * TARGETS_STEP

            def chunk(c, carry):
                rows = pl.ds(pl.multiple_of(c * ROWS, ROWS), ROWS)
                sums = [jnp.zeros((ROWS, 2 * rhs), jnp.float32) for _ in range(TARGETS_STEP)]
                for slot in range(slots):
                    value = products[slot, rows, :]
                    target = pairs_ref[0, slot]
                    for j in range(TARGETS_STEP):
                        live = (target == first + j) & (slot < count)
                        sums[j] = sums[j] + jnp.where(live, 1.0, 0.0) * value
                for j in range(TARGETS_STEP):
                    near[first + j, rows, :] = sums[j]
                return carry

            lax.fori_loop(0, box // ROWS, chunk, 0)

        @pl.when(k >= first_store)
        def _():
            for j in range(TARGETS_STEP):
                place = (k - first_store) * TARGETS_STEP + j

                @pl.when(place < boxes)
                def _():
                    for part in range(2):
                        total = section[levels - 1, place, part].astype(jnp.float32)
                        total = total + near[place, :, part * rhs : (part + 1) * rhs]
                        result[place, part] = total.astype(jnp.bfloat16)
                    store(place).start()

        return carry

    lax.fori_loop(0, steps, step, 0)

    def drain(place, carry):
        for level in range(levels):
            hop(level, place).wait_send()
        store(place).wait()
        return carry

    lax.fori_loop(0, boxes, drain, 0)

    @pl.when(has_right)
    def _():
        to_right.wait_send()

    @pl.when(has_left)
    def _():
        to_left.wait_send()


def per_device(fields, own_factor, partner_factor, near_blocks, near_pairs, near_count):
    levels, boxes, _, box, rhs = own_factor.shape[:4] + fields.shape[3:]
    slots = near_blocks.shape[0]
    devices = lax.axis_size("leaf")
    smem = pl.BlockSpec(memory_space=pltpu.SMEM)
    hbm = pl.BlockSpec(memory_space=pl.ANY)
    vector = (2, box, rhs)
    weight = (2, box, box)
    bf16, f32 = jnp.bfloat16, jnp.float32
    dma = pltpu.SemaphoreType.DMA
    products = levels * boxes * 2 + slots
    return pl.pallas_call(
        functools.partial(kernel, devices),
        out_shape=jax.ShapeDtypeStruct(fields.shape, bf16),
        in_specs=[smem, smem, hbm, hbm, hbm, hbm],
        out_specs=hbm,
        scratch_shapes=[
            pltpu.VMEM((2 * boxes,) + vector, bf16),
            pltpu.VMEM((levels, boxes) + weight, bf16),
            pltpu.VMEM((levels, boxes) + weight, bf16),
            pltpu.VMEM((slots,) + weight, bf16),
            pltpu.VMEM((levels, boxes) + vector, bf16),
            pltpu.VMEM((levels, boxes) + vector, bf16),
            pltpu.VMEM((slots, box, 2 * rhs), f32),
            pltpu.VMEM((boxes, box, 2 * rhs), f32),
            pltpu.VMEM((boxes,) + vector, bf16),
            dma((levels, boxes)),
            dma((levels, boxes)),
            dma((2,)),
            dma((2,)),
            dma((1,)),
            dma((levels,)),
            dma((levels,)),
            dma((1,)),
            dma((boxes,)),
        ],
        compiler_params=pltpu.CompilerParams(
            collective_id=0, has_side_effects=True, vmem_limit_bytes=56 * 2**20
        ),
        cost_estimate=pl.CostEstimate(
            flops=8 * products * box * box * rhs,
            bytes_accessed=(products * box * box + 2 * boxes * box * rhs) * 4,
            transcendentals=0,
        ),
    )(near_pairs.T, near_count, fields, own_factor, partner_factor, near_blocks)


def solution(mesh):
    in_specs = (
        P(("case", "leaf"), None, None, None),
        P(None, ("case", "leaf"), None, None, None),
        P(None, ("case", "leaf"), None, None, None),
        P(("case", "leaf"), None, None, None),
        P("leaf", None),
        P("leaf"),
    )
    out_specs = P(("case", "leaf"), None, None, None)
    return jax.shard_map(
        per_device, mesh=mesh, in_specs=in_specs, out_specs=out_specs, check_vma=False
    )
```
